128 devices in a mesh: row: 2 (over core), col: 2 (over x_hi), layer: 32 (over z, y, x_lo).
Axes of the slice: x: 4 (x_hi: 2, x_lo: 2; x = x_hi * 2 + x_lo), y: 4, z: 4, core: 2. Of those that a mesh axis runs over, the one named last changes fastest.
Arguments:
- flow: bfloat16 [4096, 16384], P('row', ('col', 'layer')), may hold values from 0.0099487305 to 1
- graph: bfloat16 [16384, 16384], P('col', 'layer'), may hold values from 6.0796738e-06 to 0.00024414062
- graph_pattern: int32 [128, 128], P('col', 'layer'), may hold values from 0 to 1, as said below
- out_pattern: int32 [32, 128], P(('row', 'col'), 'layer'), may hold values from 0 to 1, as said below
Outputs:
- new_flow: float32 [4096, 16384], P(('row', 'col'), 'layer')
The draws below stay inside these ranges and needn't reach their ends.
Inputs may be any that keep to these rules, and one draw needn't show every extreme that they name: Every diagonal block graph_pattern[a, a] is 1; block rows differ in density. Every block column b has out_pattern[b % 32, b] = 1.
All inputs are finite; a program needn't handle non-finite values.
Results may differ from the reference program's by a relative error of at most 0.0003.
Values may be sent and summed in bfloat16 or wider, within the bound.
A program may use at most 256 MiB of HBM per device.

```python
import math
import jax
import jax.numpy as jnp

BLOCK = 128
GRAPH_BLOCKS = 128
ORDER = 16384
ROWS = 4096
SLAB_BLOCKS = 32


def draw_graph_pattern(key, part):
    key = jax.random.fold_in(key, 11)
    first, second = jax.random.split(key)
    level = jax.random.randint(first, (GRAPH_BLOCKS, 1), 1, 8)
    rolled = jax.random.randint(second, (GRAPH_BLOCKS, GRAPH_BLOCKS), 0, 8)
    rows = jnp.arange(GRAPH_BLOCKS)[:, None]
    cols = jnp.arange(GRAPH_BLOCKS)[None, :]
    return ((rolled < level) | (rows == cols)).astype(jnp.int32)


def draw_out_pattern(key, part):
    key = jax.random.fold_in(key, 23)
    rolled = jax.random.randint(key, (SLAB_BLOCKS, GRAPH_BLOCKS), 0, 8)
    rows = jnp.arange(SLAB_BLOCKS)[:, None]
    cols = jnp.arange(GRAPH_BLOCKS)[None, :]
    return ((rolled < 4) | (cols % SLAB_BLOCKS == rows)).astype(jnp.int32)


def shard_levels(rng, dims, cuts, smallest, top_value):
    def one(axis_at, blocks):
        heights = jax.random.uniform(jax.random.fold_in(jax.random.fold_in(rng, 6), axis_at), (blocks,), jnp.float32, smallest / len(cuts), top_value / len(cuts))
        return jnp.repeat(jnp.exp(heights), dims[axis_at] // blocks).reshape((-1,) + (1,) * (len(dims) - axis_at - 1))

    level = one(*cuts[0])
    for cut in cuts[1:]:
        level = level * one(*cut)
    return level


def setup_inputs(seed: int = 0) -> dict:
    streams_of = jax.random.split(jax.random.key(seed), 5)
    flow = jnp.clip(jnp.exp(math.log(1.0) - 4.61031033 * jax.random.uniform(streams_of[0], (ROWS, ORDER), jnp.float32) ** shard_levels(streams_of[0], (ROWS, ORDER), ((0, 2), (1, 64)), -0.2, 0.2)), 0.0099487305, 1.0).astype(jnp.bfloat16)
    graph = jnp.clip(jnp.exp(math.log(0.00024414062) - 3.6927934 * jax.random.uniform(streams_of[1], (ORDER, ORDER), jnp.float32) ** shard_levels(streams_of[1], (ORDER, ORDER), ((0, 2), (1, 32)), -0.2, 0.2)), 6.079673767089844e-06, 0.00024414062).astype(jnp.bfloat16)
    graph_pattern = draw_graph_pattern(jax.random.fold_in(streams_of[4], 71), 0)
    out_pattern = draw_out_pattern(jax.random.fold_in(streams_of[4], 71), 0)
    return dict(flow=flow, graph=graph, graph_pattern=graph_pattern, out_pattern=out_pattern)


def reference(flow, graph, graph_pattern, out_pattern):
    blocked = graph.reshape(GRAPH_BLOCKS, BLOCK, GRAPH_BLOCKS, BLOCK)
    masked = (blocked * graph_pattern[:, None, :, None].astype(jnp.bfloat16)).reshape(ORDER, ORDER)
    expanded = jnp.dot(flow, masked, preferred_element_type=jnp.float32)
    keep = out_pattern[:, None, :, None].astype(jnp.float32)
    inflated = ((expanded * expanded).reshape(SLAB_BLOCKS, BLOCK, GRAPH_BLOCKS, BLOCK) * keep).reshape(ROWS, ORDER)
    totals = jnp.sum(inflated, axis=0)
    return jnp.float32(ROWS) * inflated / totals[None, :]
```

```python
import jax
import jax.numpy as jnp
from jax import lax
from jax.experimental import pallas as pl
from jax.experimental.pallas import tpu as pltpu
from jax.sharding import PartitionSpec as P

BLOCK = 128
SLABS = 8
Z = 4
Y = 4
MESH = pl.DeviceIdType.MESH


def kernel(
    flow_ref,
    graph_ref,
    gp_ref,
    op_ref,
    out_ref,
    tot_ref,
    a,
    b_own,
    b_par,
    b_out,
    own,
    c1s,
    c1r,
    c2s,
    c2r,
    c3s,
    c3r,
    sums,
    sums_in,
    g_send,
    g_recv,
    b_send,
    b_recv,
    f_send,
    f_recv,
    c_send,
    c_recv,
    o_sem,
    t_send,
    t_recv,
    l_sem,
):
    core = lax.axis_index("row")
    xh = lax.axis_index("col")
    layer = lax.axis_index("layer")
    z = layer // 8
    y = lax.rem(layer // 2, 4)
    xl = lax.rem(layer, 2)
    yn = (lax.rem(y + 1, 4), lax.rem(y + 3, 4))
    zn = (lax.rem(z + 1, 4), lax.rem(z + 3, 4))

    def at(zz, yy, xxl):
        return zz * 8 + yy * 2 + xxl

    y_dev = tuple((core, xh, at(z, v, xl)) for v in yn)
    z_dev = tuple((core, xh, at(v, y, xl)) for v in zn)
    pair = (core, xh, at(z, y, 1 - xl))
    cross = (core, 1 - xh, at(z, y, 1 - xl))
    sibling = (1 - core, xh, layer)
    opposite = (core, 1 - xh, layer)
    diagonal = (1 - core, 1 - xh, layer)
    peers = (sibling, opposite, diagonal)

    load_a = pltpu.make_async_copy(flow_ref, a.at[:, :, z, y], l_sem.at[0])
    load_a.start()
    load_bo = pltpu.make_async_copy(graph_ref.at[pl.ds(core * 8, 8), 1 - xl], b_out, l_sem.at[1])
    load_bo.start()
    load_b = pltpu.make_async_copy(graph_ref.at[:, xl], b_own, l_sem.at[2])
    load_b.start()

    barrier = pltpu.get_barrier_semaphore()
    for dev in (*y_dev, *z_dev, pair, cross, *peers):
        pl.semaphore_signal(barrier, inc=1, device_id=dev, device_id_type=MESH)
    pl.semaphore_wait(barrier, 9)

    def gather_copy(stage, f, d, s):
        first = y_dev if f == 0 else z_dev
        second = z_dev if f == 0 else y_dev
        back = 1 - d
        rows = pl.ds(64 * d, 64)
        if stage == 0:
            ref, dev = a.at[f, s, z, y], first[d]
        elif stage == 1:
            ref = a.at[f, s, z, yn[back], rows] if f == 0 else a.at[f, s, zn[back], y, rows]
            dev = first[d]
        elif stage == 2:
            ref = a.at[f, s, z] if f == 0 else a.at[f, s, :, y]
            dev = second[d]
        else:
            ref = a.at[f, s, zn[back], :, rows] if f == 0 else a.at[f, s, :, yn[back], rows]
            dev = second[d]
        return pltpu.make_async_remote_copy(
            src_ref=ref,
            dst_ref=ref,
            send_sem=g_send.at[stage, f, d, s],
            recv_sem=g_recv.at[stage, f, d, s],
            device_id=dev,
            device_id_type=MESH,
        )

    def remote(src, dst, send, recv, dev):
        return pltpu.make_async_remote_copy(
            src_ref=src, dst_ref=dst, send_sem=send, recv_sem=recv, device_id=dev, device_id_type=MESH
        )

    def issue(stage, s):
        for d in range(2):
            for f in range(2):
                if stage > 0:
                    if stage == 2 and d == 0:
                        gather_copy(1, f, 0, s).wait_recv()
                        gather_copy(1, f, 1, s).wait_recv()
                    elif stage != 2:
                        gather_copy(stage - 1, f, d, s).wait_recv()
                gather_copy(stage, f, d, s).start()

    def b_copy(j):
        return remote(b_out.at[j], b_par.at[core * 8 + j], b_send.at[j], b_recv.at[j], pair)

    def f_copy(j):
        ref = b_par.at[core * 8 + j]
        return remote(ref, ref, f_send.at[j], f_recv.at[j], sibling)

    def c_copy(k, s):
        src, dst, dev = ((c1s, c1r, cross), (c2s, c2r, pair), (c3s, c3r, cross))[k]
        return remote(src.at[s], dst.at[s], c_send.at[k, s], c_recv.at[k, s], dev)

    def out_copy(s):
        return pltpu.make_async_copy(own.at[s], out_ref.at[s], o_sem.at[s])

    def mask(ref, j, chunk, x):
        for r in range(2):
            for c in range(4):
                keep = gp_ref[(chunk * 2 + x) * 2 + r, c].astype(jnp.float32)
                rows, cols = pl.ds(r * BLOCK, BLOCK), pl.ds(c * BLOCK, BLOCK)
                ref[j, rows, cols] = (ref[j, rows, cols].astype(jnp.float32) * keep).astype(jnp.bfloat16)

    def rows_of(s):
        halves = []
        for h in (xh, 1 - xh):
            halves.append(jnp.concatenate([a[h, s, zz, yy] for zz in range(Z) for yy in range(Y)], axis=1))
        return jnp.concatenate(halves, axis=0)

    def product(s, b, n):
        cols = pl.ds(pl.multiple_of(n * 256, 256), 256)
        return jnp.dot(rows_of(s), b[:, :, cols].reshape(4096, 256), preferred_element_type=jnp.float32), cols

    def compute_own(s):
        @pl.loop(0, 2)
        def _(n):
            r, cols = product(s, b_own, n)
            own[s, :, cols] = r[:BLOCK]
            c1s[s, :, cols] = r[BLOCK:]

        c_copy(0, s).start()

    def compute_par(s):
        c_copy(0, s).wait_recv()

        @pl.loop(0, 2)
        def _(n):
            r, cols = product(s, b_par, n)
            c2s[s, :, cols] = r[:BLOCK] + c1r[s, :, cols]
            c3s[s, :, cols] = r[BLOCK:]

        c_copy(1, s).start()
        c_copy(2, s).start()

    def finish(s):
        c_copy(1, s).wait_recv()
        c_copy(2, s).wait_recv()
        for c in range(4):
            cols = pl.ds(c * BLOCK, BLOCK)
            keep = op_ref[s, c].astype(jnp.float32)
            v = own[s, :, cols] + c2r[s, :, cols] + c3r[s, :, cols]
            v = v * v * keep
            own[s, :, cols] = v
            sums[:, cols] += v.reshape(16, 8, BLOCK).sum(axis=0)
        out_copy(s).start()

    sums[...] = jnp.zeros_like(sums)
    load_a.wait()
    issue(0, 0)
    load_bo.wait()

    @pl.loop(0, 8)
    def _(j):
        mask(b_out, j, core * 8 + j, 1 - xl)
        b_copy(j).start()

    last = SLABS + 4

    def par_end(t):
        return jnp.clip(jnp.minimum(t - 3, 2 * (t - 6)), 0, SLABS)

    def fwd_end(t):
        return jnp.clip(2 * (t - 3) + 1, 0, 8)

    @pl.loop(1, last)
    def _(t):
        for stage in (3, 2, 1, 0):
            s = t - stage

            @pl.when((s >= 0) & (s < SLABS))
            def _():
                issue(stage, s)

        @pl.when(t == 3)
        def _():
            load_b.wait()

            @pl.loop(0, 16)
            def _(j):
                mask(b_own, j, j, xl)

        @pl.loop(fwd_end(t - 1), fwd_end(t))
        def _(j):
            b_copy(j).wait_recv()
            f_copy(j).start()

        @pl.when(t >= 4)
        def _():
            s = t - 4
            for f in range(2):
                for d in range(2):
                    gather_copy(3, f, d, s).wait_recv()
            compute_own(s)

        @pl.when(t == 7)
        def _():
            @pl.loop(0, 8)
            def _(j):
                f_copy(j).wait_recv()

        @pl.loop(par_end(t - 1), par_end(t))
        def _(s):
            compute_par(s)

        @pl.loop(par_end(t - 2), par_end(t - 1))
        def _(s):
            finish(s)

    @pl.loop(par_end(last - 2), par_end(last - 1))
    def _(s):
        finish(s)

    for k, dev in enumerate(peers):
        remote(sums, sums_in.at[k], t_send.at[k], t_recv.at[k], dev).start()

    @pl.loop(0, SLABS)
    def _(s):
        for stage in range(4):
            for f in range(2):
                for d in range(2):
                    gather_copy(stage, f, d, s).wait_send()
        for k in range(3):
            c_copy(k, s).wait_send()
        b_copy(s).wait_send()
        f_copy(s).wait_send()
        out_copy(s).wait()

    for k, dev in enumerate(peers):
        remote(sums, sums_in.at[k], t_send.at[k], t_recv.at[k], dev).wait()
    total = sums[...] + sums_in[0] + sums_in[1] + sums_in[2]
    tot_ref[...] = jnp.broadcast_to(total.sum(axis=0, keepdims=True), total.shape)


def shards(flow, graph, graph_pattern, out_pattern):
    f32, bf16 = jnp.float32, jnp.bfloat16
    dma = pltpu.SemaphoreType.DMA
    part = pltpu.VMEM((SLABS, BLOCK, 512), f32)
    inflated, totals = pl.pallas_call(
        kernel,
        out_shape=(
            jax.ShapeDtypeStruct((SLABS, BLOCK, 512), f32),
            jax.ShapeDtypeStruct((8, 512), f32),
        ),
        in_specs=[
            pl.BlockSpec(memory_space=pl.ANY),
            pl.BlockSpec(memory_space=pl.ANY),
            pl.BlockSpec(memory_space=pltpu.SMEM),
            pl.BlockSpec(memory_space=pltpu.SMEM),
        ],
        out_specs=(pl.BlockSpec(memory_space=pl.ANY), pl.BlockSpec(memory_space=pltpu.VMEM)),
        scratch_shapes=[
            pltpu.VMEM((2, SLABS, Z, Y, BLOCK, 256), bf16),
            pltpu.VMEM((16, 256, 512), bf16),
            pltpu.VMEM((16, 256, 512), bf16),
            pltpu.VMEM((8, 256, 512), bf16),
            part,
            part,
            part,
            part,
            part,
            part,
            part,
            pltpu.VMEM((8, 512), f32),
            pltpu.VMEM((3, 8, 512), f32),
            dma((4, 2, 2, SLABS)),
            dma((4, 2, 2, SLABS)),
            dma((8,)),
            dma((8,)),
            dma((8,)),
            dma((8,)),
            dma((3, SLABS)),
            dma((3, SLABS)),
            dma((SLABS,)),
            dma((3,)),
            dma((3,)),
            dma((3,)),
        ],
        compiler_params=pltpu.CompilerParams(
            collective_id=0, has_side_effects=True, vmem_limit_bytes=56 * 1024 * 1024
        ),
        cost_estimate=pl.CostEstimate(flops=2 * 2048 * 4096 * 1024, bytes_accessed=12 << 20, transcendentals=0),
    )(
        flow.reshape(2, SLABS, BLOCK, 256),
        graph.reshape(16, 2, 256, 512),
        graph_pattern,
        out_pattern,
    )
    return (jnp.float32(4096) * inflated / totals[0]).reshape(SLABS * BLOCK, 512)


def solution(mesh):
    placed = (
        P("row", ("col", "layer")),
        P("col", "layer"),
        P("col", "layer"),
        P(("row", "col"), "layer"),
    )
    return jax.shard_map(
        shards, mesh=mesh, in_specs=placed, out_specs=P(("row", "col"), "layer"), check_vma=False
    )
```

```python
import jax
import jax.numpy as jnp
from jax import lax
from jax.experimental import pallas as pl
from jax.experimental.pallas import tpu as pltpu
from jax.sharding import PartitionSpec as P

BLOCK = 128
ROWS = 4096
SLABS = 16
HEIGHT = 1024 // SLABS
HALF = HEIGHT // 2
AHEAD = 3
LAG = 2
FORWARD_FROM = 7
PARTNER_FROM = 15
CODES = 65534.0
Z = 4
Y = 4
MESH = pl.DeviceIdType.MESH


def kernel(
    flow_ref,
    graph_ref,
    gp_ref,
    out_ref,
    factor_ref,
    a,
    b_own,
    b_par,
    b_out,
    own,
    c1s,
    c1r,
    c2s,
    c2r,
    c3s,
    c3r,
    m1s,
    m1r,
    m2s,
    m2r,
    m3s,
    m3r,
    gp,
    sums,
    sums_in,
    g_send,
    g_recv,
    b_send,
    b_recv,
    f_send,
    f_recv,
    c_send,
    c_recv,
    m_send,
    m_recv,
    o_sem,
    t_send,
    t_recv,
    l_sem,
):
    core = lax.axis_index("row")
    xh = lax.axis_index("col")
    layer = lax.axis_index("layer")
    z = layer // 8
    y = lax.rem(layer // 2, 4)
    xl = lax.rem(layer, 2)
    yn = (lax.rem(y + 1, 4), lax.rem(y + 3, 4))
    zn = (lax.rem(z + 1, 4), lax.rem(z + 3, 4))

    def at(zz, yy, xxl):
        return zz * 8 + yy * 2 + xxl

    y_dev = tuple((core, xh, at(z, v, xl)) for v in yn)
    z_dev = tuple((core, xh, at(v, y, xl)) for v in zn)
    pair = (core, xh, at(z, y, 1 - xl))
    cross = (core, 1 - xh, at(z, y, 1 - xl))
    sibling = (1 - core, xh, layer)
    opposite = (core, 1 - xh, layer)
    diagonal = (1 - core, 1 - xh, layer)
    peers = (sibling, opposite, diagonal)

    load_a = pltpu.make_async_copy(flow_ref, a.at[:, :, z, y], l_sem.at[0])
    load_a.start()
    load_bo = pltpu.make_async_copy(graph_ref.at[pl.ds(core * 8, 8), 1 - xl], b_out, l_sem.at[1])
    load_bo.start()
    load_gp = pltpu.make_async_copy(gp_ref, gp, l_sem.at[3])
    load_gp.start()
    load_b = pltpu.make_async_copy(graph_ref.at[:, xl], b_own, l_sem.at[2])
    load_b.start()

    barrier = pltpu.get_barrier_semaphore()
    for dev in (*y_dev, *z_dev, pair, cross, *peers):
        pl.semaphore_signal(barrier, inc=1, device_id=dev, device_id_type=MESH)
    pl.semaphore_wait(barrier, 9)

    def gather_copy(stage, f, d, s):
        first = y_dev if f == 0 else z_dev
        second = z_dev if f == 0 else y_dev
        back = 1 - d
        rows = pl.ds(HALF * d, HALF)
        if stage == 0:
            ref, dev = a.at[f, s, z, y], first[d]
        elif stage == 1:
            ref = a.at[f, s, z, yn[back], rows] if f == 0 else a.at[f, s, zn[back], y, rows]
            dev = first[d]
        elif stage == 2:
            ref = a.at[f, s, z] if f == 0 else a.at[f, s, :, y]
            dev = second[d]
        else:
            ref = a.at[f, s, zn[back], :, rows] if f == 0 else a.at[f, s, :, yn[back], rows]
            dev = second[d]
        return pltpu.make_async_remote_copy(
            src_ref=ref,
            dst_ref=ref,
            send_sem=g_send.at[stage, f, d, s],
            recv_sem=g_recv.at[stage, f, d, s],
            device_id=dev,
            device_id_type=MESH,
        )

    def remote(src, dst, send, recv, dev):
        return pltpu.make_async_remote_copy(
            src_ref=src, dst_ref=dst, send_sem=send, recv_sem=recv, device_id=dev, device_id_type=MESH
        )

    def issue(stage, s):
        for d in range(2):
            for f in range(2):
                if stage > 0:
                    if stage == 2 and d == 0:
                        gather_copy(1, f, 0, s).wait_recv()
                        gather_copy(1, f, 1, s).wait_recv()
                    elif stage != 2:
                        gather_copy(stage - 1, f, d, s).wait_recv()
                gather_copy(stage, f, d, s).start()

    def b_copy(j):
        return remote(b_out.at[j], b_par.at[core * 8 + j], b_send.at[j], b_recv.at[j], pair)

    def f_copy(j):
        ref = b_par.at[core * 8 + j]
        return remote(ref, ref, f_send.at[j], f_recv.at[j], sibling)

    parts = ((c1s, c1r, m1s, m1r, cross), (c2s, c2r, m2s, m2r, pair), (c3s, c3r, m3s, m3r, cross))

    def c_copies(k, s):
        src, dst, top, top_in, dev = parts[k]
        return (
            remote(src.at[s], dst.at[s], c_send.at[k, s], c_recv.at[k, s], dev),
            remote(top.at[s], top_in.at[s], m_send.at[k, s], m_recv.at[k, s], dev),
        )

    def encode(k, s, cols, v):
        top = jnp.maximum(v.max(axis=0, keepdims=True), 1e-30)
        code = (v * (CODES / top) + 0.5).astype(jnp.int32) - 32767
        parts[k][0][s, :, cols] = code.astype(jnp.int16)
        parts[k][2][s, :, cols] = top

    def decode(k, s, cols):
        code = parts[k][1][s, :, cols].astype(jnp.int32) + 32767
        return code.astype(jnp.float32) * (parts[k][3][s, :, cols] * (1.0 / CODES))

    def out_copy(s):
        return pltpu.make_async_copy(own.at[s], out_ref.at[s], o_sem.at[s])

    def mask(ref, j, chunk, x):
        for r in range(2):
            for c in range(4):
                keep = gp[(chunk * 2 + x) * 2 + r, c].astype(jnp.float32)
                keep = jnp.full((16, BLOCK), keep, jnp.float32).astype(jnp.bfloat16)
                rows, cols = pl.ds(r * BLOCK, BLOCK), pl.ds(c * BLOCK, BLOCK)
                block = ref[j, rows, cols].reshape(8, 16, BLOCK) * keep
                ref[j, rows, cols] = block.reshape(BLOCK, BLOCK)

    def rows_of(s):
        halves = []
        for h in (xh, 1 - xh):
            halves.append(jnp.concatenate([a[h, s, zz, yy] for zz in range(Z) for yy in range(Y)], axis=1))
        return jnp.concatenate(halves, axis=0)

    def product(s, b, n):
        cols = pl.ds(pl.multiple_of(n * 256, 256), 256)
        return jnp.dot(rows_of(s), b[:, :, cols].reshape(4096, 256), preferred_element_type=jnp.float32), cols

    def compute_own(s):
        @pl.loop(0, 2)
        def _(n):
            r, cols = product(s, b_own, n)
            own[s, :, cols] = r[:HEIGHT]
            encode(0, s, cols, r[HEIGHT:])

        for copy in c_copies(0, s):
            copy.start()

    def compute_par(s):
        for copy in c_copies(0, s):
            copy.wait_recv()

        @pl.loop(0, 2)
        def _(n):
            r, cols = product(s, b_par, n)
            encode(1, s, cols, r[:HEIGHT] + decode(0, s, cols))
            encode(2, s, cols, r[HEIGHT:])

        for k in (1, 2):
            for copy in c_copies(k, s):
                copy.start()

    def finish(s):
        for k in (1, 2):
            for copy in c_copies(k, s):
                copy.wait_recv()
        for c in range(4):
            cols = pl.ds(c * BLOCK, BLOCK)
            keep = gp[64 + s * HEIGHT // BLOCK, c].astype(jnp.float32)
            v = own[s, :, cols] + decode(1, s, cols) + decode(2, s, cols)
            v = v * v * keep
            own[s, :, cols] = v
            sums[:, cols] += v.reshape(HEIGHT // 8, 8, BLOCK).sum(axis=0)
        out_copy(s).start()

    sums[...] = jnp.zeros_like(sums)
    load_a.wait()

    @pl.loop(0, AHEAD + 1)
    def _(s):
        issue(0, s)

    load_bo.wait()
    load_gp.wait()
    load_b.wait()

    def send_b(j):
        mask(b_out, j, core * 8 + j, 1 - xl)
        b_copy(j).start()

    send_b(0)
    last = SLABS + 4 * LAG + 1

    def par_end(t):
        return jnp.clip(jnp.minimum(t - 4 * LAG, 3 * (t - PARTNER_FROM + 1)), 0, SLABS)

    def fwd_end(t):
        return jnp.clip(t - FORWARD_FROM, 0, 8)

    @pl.loop(1, last)
    def _(t):
        for stage in (3, 2, 1, 0):
            s = t - LAG * stage + (AHEAD if stage == 0 else 0)

            @pl.when((s >= 0) & (s < SLABS))
            def _():
                issue(stage, s)

        @pl.when(t < 8)
        def _():
            send_b(t)

        @pl.when(t < 5)
        def _():
            @pl.loop(4 * (t - 1), 4 * t)
            def _(j):
                mask(b_own, j, j, xl)

        @pl.loop(fwd_end(t - 1), fwd_end(t))
        def _(j):
            b_copy(j).wait_recv()
            f_copy(j).start()

        @pl.when((t >= 4 * LAG) & (t < SLABS + 4 * LAG))
        def _():
            s = t - 4 * LAG
            for f in range(2):
                for d in range(2):
                    gather_copy(3, f, d, s).wait_recv()
            compute_own(s)

        @pl.when(t == PARTNER_FROM)
        def _():
            @pl.loop(0, 8)
            def _(j):
                f_copy(j).wait_recv()

        @pl.loop(par_end(t - 1), par_end(t))
        def _(s):
            compute_par(s)

        @pl.loop(par_end(t - 3), par_end(t - 2))
        def _(s):
            finish(s)

    @pl.loop(par_end(last - 3), par_end(last - 1))
    def _(s):
        finish(s)

    for k, dev in enumerate(peers):
        remote(sums, sums_in.at[k], t_send.at[k], t_recv.at[k], dev).start()

    @pl.loop(0, SLABS)
    def _(s):
        for stage in range(4):
            for f in range(2):
                for d in range(2):
                    gather_copy(stage, f, d, s).wait_send()
        for k in range(3):
            for copy in c_copies(k, s):
                copy.wait_send()
        out_copy(s).wait()

    @pl.loop(0, 8)
    def _(j):
        b_copy(j).wait_send()
        f_copy(j).wait_send()

    for k, dev in enumerate(peers):
        remote(sums, sums_in.at[k], t_send.at[k], t_recv.at[k], dev).wait()
    total = sums[...] + sums_in[0] + sums_in[1] + sums_in[2]
    factor_ref[...] = jnp.float32(ROWS) / total.sum(axis=0, keepdims=True)


def shards(flow, graph, graph_pattern, out_pattern):
    f32, bf16 = jnp.float32, jnp.bfloat16
    dma = pltpu.SemaphoreType.DMA
    part = pltpu.VMEM((SLABS, HEIGHT, 512), jnp.int16)
    tops = pltpu.VMEM((SLABS, 1, 512), f32)
    inflated, factor = pl.pallas_call(
        kernel,
        out_shape=(
            jax.ShapeDtypeStruct((SLABS, HEIGHT, 512), f32),
            jax.ShapeDtypeStruct((1, 512), f32),
        ),
        in_specs=[
            pl.BlockSpec(memory_space=pl.ANY),
            pl.BlockSpec(memory_space=pl.ANY),
            pl.BlockSpec(memory_space=pl.ANY),
        ],
        out_specs=(pl.BlockSpec(memory_space=pl.ANY), pl.BlockSpec(memory_space=pltpu.VMEM)),
        scratch_shapes=[
            pltpu.VMEM((2, SLABS, Z, Y, HEIGHT, 256), bf16),
            pltpu.VMEM((16, 256, 512), bf16),
            pltpu.VMEM((16, 256, 512), bf16),
            pltpu.VMEM((8, 256, 512), bf16),
            pltpu.VMEM((SLABS, HEIGHT, 512), f32),
            part,
            part,
            part,
            part,
            part,
            part,
            tops,
            tops,
            tops,
            tops,
            tops,
            tops,
            pltpu.SMEM((72, 4), jnp.int32),
            pltpu.VMEM((8, 512), f32),
            pltpu.VMEM((3, 8, 512), f32),
            dma((4, 2, 2, SLABS)),
            dma((4, 2, 2, SLABS)),
            dma((8,)),
            dma((8,)),
            dma((8,)),
            dma((8,)),
            dma((3, SLABS)),
            dma((3, SLABS)),
            dma((3, SLABS)),
            dma((3, SLABS)),
            dma((SLABS,)),
            dma((3,)),
            dma((3,)),
            dma((4,)),
        ],
        compiler_params=pltpu.CompilerParams(
            collective_id=0, has_side_effects=True, vmem_limit_bytes=56 * 1024 * 1024
        ),
        cost_estimate=pl.CostEstimate(flops=2 * 2048 * 4096 * 1024, bytes_accessed=12 << 20, transcendentals=0),
    )(
        flow.reshape(2, SLABS, HEIGHT, 256),
        graph.reshape(16, 2, 256, 512),
        jnp.concatenate([graph_pattern, out_pattern]),
    )
    return inflated.reshape(SLABS * HEIGHT, 512) * factor


def solution(mesh):
    placed = (
        P("row", ("col", "layer")),
        P("col", "layer"),
        P("col", "layer"),
        P(("row", "col"), "layer"),
    )
    return jax.shard_map(
        shards, mesh=mesh, in_specs=placed, out_specs=P(("row", "col"), "layer"), check_vma=False
    )
```

```python
import jax
import jax.numpy as jnp
from jax import lax
from jax.experimental import pallas as pl
from jax.experimental.pallas import tpu as pltpu
from jax.sharding import PartitionSpec as P

BLOCK = 128
ROWS = 4096
SLABS = 16
HEIGHT = 1024 // SLABS
HALF = HEIGHT // 2
AHEAD = 3
LAG = 2
FORWARD_FROM = 5
PARTNER_FROM = 13
CODES = 65534.0
Z = 4
Y = 4
MESH = pl.DeviceIdType.MESH


def kernel(
    flow_ref,
    graph_ref,
    gp_ref,
    op_ref,
    out_ref,
    factor_ref,
    a,
    b_own,
    b_par,
    b_out,
    own,
    c1s,
    c1r,
    c2s,
    c2r,
    c3s,
    c3r,
    m1s,
    m1r,
    m2s,
    m2r,
    m3s,
    m3r,
    gp,
    op,
    sums,
    sums_in,
    g_send,
    g_recv,
    b_send,
    b_recv,
    f_send,
    f_recv,
    c_send,
    c_recv,
    m_send,
    m_recv,
    o_sem,
    t_send,
    t_recv,
    l_sem,
):
    core = lax.axis_index("row")
    xh = lax.axis_index("col")
    layer = lax.axis_index("layer")
    z = layer // 8
    y = lax.rem(layer // 2, 4)
    xl = lax.rem(layer, 2)
    yn = (lax.rem(y + 1, 4), lax.rem(y + 3, 4))
    zn = (lax.rem(z + 1, 4), lax.rem(z + 3, 4))

    def at(zz, yy, xxl):
        return zz * 8 + yy * 2 + xxl

    y_dev = tuple((core, xh, at(z, v, xl)) for v in yn)
    z_dev = tuple((core, xh, at(v, y, xl)) for v in zn)
    pair = (core, xh, at(z, y, 1 - xl))
    cross = (core, 1 - xh, at(z, y, 1 - xl))
    sibling = (1 - core, xh, layer)
    opposite = (core, 1 - xh, layer)
    diagonal = (1 - core, 1 - xh, layer)
    peers = (sibling, opposite, diagonal)

    barrier = pltpu.get_barrier_semaphore()
    for dev in (*y_dev, *z_dev, pair, cross, *peers):
        pl.semaphore_signal(barrier, inc=1, device_id=dev, device_id_type=MESH)

    load_a = pltpu.make_async_copy(flow_ref, a.at[:, :, z, y], l_sem.at[0])
    load_a.start()
    load_bo = pltpu.make_async_copy(graph_ref.at[pl.ds(core * 8, 8), 1 - xl], b_out, l_sem.at[1])
    load_bo.start()
    load_gp = pltpu.make_async_copy(gp_ref, gp, l_sem.at[3])
    load_gp.start()
    load_op = pltpu.make_async_copy(op_ref, op, l_sem.at[4])
    load_op.start()
    load_b = pltpu.make_async_copy(graph_ref.at[:, xl], b_own, l_sem.at[2])
    load_b.start()

    pl.semaphore_wait(barrier, 9)

    def gather_copy(stage, f, d, s):
        first = y_dev if f == 0 else z_dev
        second = z_dev if f == 0 else y_dev
        back = 1 - d
        rows = pl.ds(HALF * d, HALF)
        if stage == 0:
            ref, src, dev = a.at[f, s, z, y], flow_ref.at[f, s], first[d]
        elif stage == 1:
            ref = a.at[f, s, z, yn[back], rows] if f == 0 else a.at[f, s, zn[back], y, rows]
            dev = first[d]
        elif stage == 2:
            ref = a.at[f, s, z] if f == 0 else a.at[f, s, :, y]
            dev = second[d]
        else:
            ref = a.at[f, s, zn[back], :, rows] if f == 0 else a.at[f, s, :, yn[back], rows]
            dev = second[d]
        return pltpu.make_async_remote_copy(
            src_ref=src if stage == 0 else ref,
            dst_ref=ref,
            send_sem=g_send.at[stage, f, d, s],
            recv_sem=g_recv.at[stage, f, d, s],
            device_id=dev,
            device_id_type=MESH,
        )

    def remote(src, dst, send, recv, dev):
        return pltpu.make_async_remote_copy(
            src_ref=src, dst_ref=dst, send_sem=send, recv_sem=recv, device_id=dev, device_id_type=MESH
        )

    def issue(stage, s):
        for d in range(2):
            for f in range(2):
                if stage > 0:
                    if stage == 2 and d == 0:
                        gather_copy(1, f, 0, s).wait_recv()
                        gather_copy(1, f, 1, s).wait_recv()
                    elif stage != 2:
                        gather_copy(stage - 1, f, d, s).wait_recv()
                gather_copy(stage, f, d, s).start()

    def drain(s):
        for stage in range(4):
            for f in range(2):
                for d in range(2):
                    gather_copy(stage, f, d, s).wait_send()

    def b_copy(j):
        return remote(b_out.at[j], b_par.at[core * 8 + j], b_send.at[j], b_recv.at[j], pair)

    def f_copy(j):
        ref = b_par.at[core * 8 + j]
        return remote(ref, ref, f_send.at[j], f_recv.at[j], sibling)

    parts = ((c1s, c1r, m1s, m1r, cross), (c2s, c2r, m2s, m2r, pair), (c3s, c3r, m3s, m3r, cross))

    def c_copies(k, s, direct=False):
        src, dst, top, top_in, dev = parts[k]
        if direct:
            dev = opposite
        return (
            remote(src.at[s], dst.at[s], c_send.at[k, s], c_recv.at[k, s], dev),
            remote(top.at[s], top_in.at[s], m_send.at[k, s], m_recv.at[k, s], dev),
        )

    def encode(k, s, cols, v):
        top = jnp.maximum(v.max(axis=0, keepdims=True), 1e-30)
        code = (v * (CODES / top) + 0.5).astype(jnp.int32) - 32767
        parts[k][0][s, :, cols] = code.astype(jnp.int16)
        parts[k][2][s, :, cols] = top

    def decode(k, s, cols):
        code = parts[k][1][s, :, cols].astype(jnp.int32) + 32767
        return code.astype(jnp.float32) * (parts[k][3][s, :, cols] * (1.0 / CODES))

    def out_copy(s):
        return pltpu.make_async_copy(own.at[s], out_ref.at[s], o_sem.at[s])

    def mask(ref, j, chunk, x):
        for r in range(2):
            for c in range(4):
                keep = gp[c, (chunk * 2 + x) * 2 + r].astype(jnp.float32)
                keep = jnp.full((16, BLOCK), keep, jnp.float32).astype(jnp.bfloat16)
                rows, cols = pl.ds(r * BLOCK, BLOCK), pl.ds(c * BLOCK, BLOCK)
                block = ref[j, rows, cols].reshape(8, 16, BLOCK) * keep
                ref[j, rows, cols] = block.reshape(BLOCK, BLOCK)

    def rows_of(s):
        halves = []
        for h in (xh, 1 - xh):
            halves.append(jnp.concatenate([a[h, s, zz, yy] for zz in range(Z) for yy in range(Y)], axis=1))
        return jnp.concatenate(halves, axis=0)

    def product(s, b, n):
        cols = pl.ds(pl.multiple_of(n * 256, 256), 256)
        return jnp.dot(rows_of(s), b[:, :, cols].reshape(4096, 256), preferred_element_type=jnp.float32), cols

    def compute_own(s, direct=False):
        @pl.loop(0, 2)
        def _(n):
            r, cols = product(s, b_own, n)
            own[s, :, cols] = r[:HEIGHT]
            encode(0, s, cols, r[HEIGHT:])

        for copy in c_copies(0, s, direct):
            copy.start()

    def compute_par(s, direct=False):
        if not direct:
            for copy in c_copies(0, s):
                copy.wait_recv()

        @pl.loop(0, 2)
        def _(n):
            r, cols = product(s, b_par, n)
            encode(1, s, cols, r[:HEIGHT] if direct else r[:HEIGHT] + decode(0, s, cols))
            encode(2, s, cols, r[HEIGHT:])

        for k in (1, 2):
            for copy in c_copies(k, s):
                copy.start()

    def finish(s, direct=False):
        came = (1, 2, 0) if direct else (1, 2)
        for k in came:
            for copy in c_copies(k, s, direct and k == 0):
                copy.wait_recv()
        for c in range(4):
            cols = pl.ds(c * BLOCK, BLOCK)
            keep = op[c, s * HEIGHT // BLOCK].astype(jnp.float32)
            v = own[s, :, cols] + sum(decode(k, s, cols) for k in came)
            v = v * v * keep
            own[s, :, cols] = v
            sums[:, cols] += v.reshape(HEIGHT // 8, 8, BLOCK).sum(axis=0)
        out_copy(s).start()
        for k in range(3):
            for copy in c_copies(k, s, direct and k == 0):
                copy.wait_send()

    sums[...] = jnp.zeros_like(sums)

    @pl.loop(0, AHEAD + 1)
    def _(s):
        issue(0, s)

    load_bo.wait()
    load_a.wait()
    load_gp.wait()
    load_op.wait()
    load_b.wait()

    def send_b(j):
        mask(b_out, j, core * 8 + j, 1 - xl)
        b_copy(j).start()

    send_b(0)
    last = SLABS + 4 * LAG

    def par_end(t):
        return jnp.clip(jnp.minimum(t - 4 * LAG, 4 * (t - PARTNER_FROM + 1)), 0, SLABS)

    def fwd_end(t):
        return jnp.clip(t - FORWARD_FROM, 0, 8)

    @pl.loop(1, last)
    def _(t):
        for stage in (3, 2, 1, 0):
            s = t - LAG * stage + (AHEAD if stage == 0 else 0)

            @pl.when((s >= 0) & (s < SLABS))
            def _():
                issue(stage, s)

        @pl.when(t < 8)
        def _():
            send_b(t)

        @pl.when(t < 5)
        def _():
            @pl.loop(4 * (t - 1), 4 * t)
            def _(j):
                mask(b_own, j, j, xl)

        @pl.loop(fwd_end(t - 1), fwd_end(t))
        def _(j):
            b_copy(j).wait_recv()
            f_copy(j).start()

        @pl.when((t >= 4 * LAG) & (t < last - 1))
        def _():
            s = t - 4 * LAG
            for f in range(2):
                for d in range(2):
                    gather_copy(3, f, d, s).wait_recv()
            compute_own(s)

        @pl.when(t == PARTNER_FROM)
        def _():
            @pl.loop(0, 8)
            def _(j):
                f_copy(j).wait_recv()

        @pl.loop(par_end(t - 1), par_end(t))
        def _(s):
            compute_par(s)

        @pl.loop(par_end(t - 3), par_end(t - 2))
        def _(s):
            finish(s)

        @pl.when(t > 4 * LAG)
        def _():
            drain(t - 4 * LAG - 1)

        @pl.when(t == PARTNER_FROM + 1)
        def _():
            @pl.loop(0, 8)
            def _(j):
                b_copy(j).wait_send()
                f_copy(j).wait_send()

    for f in range(2):
        for d in range(2):
            gather_copy(3, f, d, SLABS - 1).wait_recv()
    compute_own(SLABS - 1, True)
    compute_par(SLABS - 1, True)

    @pl.loop(par_end(last - 3), SLABS - 1)
    def _(s):
        finish(s)

    finish(SLABS - 1, True)

    for k, dev in enumerate(peers):
        remote(sums, sums_in.at[k], t_send.at[k], t_recv.at[k], dev).start()

    drain(SLABS - 1)

    @pl.loop(0, SLABS)
    def _(s):
        out_copy(s).wait()

    for k, dev in enumerate(peers):
        remote(sums, sums_in.at[k], t_send.at[k], t_recv.at[k], dev).wait()
    total = sums[...] + sums_in[0] + sums_in[1] + sums_in[2]
    factor_ref[...] = jnp.float32(ROWS) / total.sum(axis=0, keepdims=True)


def shards(flow, graph, graph_pattern, out_pattern):
    f32, bf16 = jnp.float32, jnp.bfloat16
    dma = pltpu.SemaphoreType.DMA
    part = pltpu.VMEM((SLABS, HEIGHT, 512), jnp.int16)
    tops = pltpu.VMEM((SLABS, 1, 512), f32)
    inflated, factor = pl.pallas_call(
        kernel,
        out_shape=(
            jax.ShapeDtypeStruct((SLABS, HEIGHT, 512), f32),
            jax.ShapeDtypeStruct((1, 512), f32),
        ),
        in_specs=[
            pl.BlockSpec(memory_space=pl.ANY),
            pl.BlockSpec(memory_space=pl.ANY),
            pl.BlockSpec(memory_space=pl.ANY),
            pl.BlockSpec(memory_space=pl.ANY),
        ],
        out_specs=(pl.BlockSpec(memory_space=pl.ANY), pl.BlockSpec(memory_space=pltpu.VMEM)),
        scratch_shapes=[
            pltpu.VMEM((2, SLABS, Z, Y, HEIGHT, 256), bf16),
            pltpu.VMEM((16, 256, 512), bf16),
            pltpu.VMEM((16, 256, 512), bf16),
            pltpu.VMEM((8, 256, 512), bf16),
            pltpu.VMEM((SLABS, HEIGHT, 512), f32),
            part,
            part,
            part,
            part,
            part,
            part,
            tops,
            tops,
            tops,
            tops,
            tops,
            tops,
            pltpu.SMEM((4, 64), jnp.int32),
            pltpu.SMEM((4, 8), jnp.int32),
            pltpu.VMEM((8, 512), f32),
            pltpu.VMEM((3, 8, 512), f32),
            dma((4, 2, 2, SLABS)),
            dma((4, 2, 2, SLABS)),
            dma((8,)),
            dma((8,)),
            dma((8,)),
            dma((8,)),
            dma((3, SLABS)),
            dma((3, SLABS)),
            dma((3, SLABS)),
            dma((3, SLABS)),
            dma((SLABS,)),
            dma((3,)),
            dma((3,)),
            dma((5,)),
        ],
        compiler_params=pltpu.CompilerParams(
            collective_id=0, has_side_effects=True, vmem_limit_bytes=56 * 1024 * 1024
        ),
        cost_estimate=pl.CostEstimate(flops=2 * 2048 * 4096 * 1024, bytes_accessed=12 << 20, transcendentals=0),
    )(
        flow.reshape(2, SLABS, HEIGHT, 256),
        graph.reshape(16, 2, 256, 512),
        graph_pattern.T,
        out_pattern.T,
    )
    return inflated.reshape(SLABS * HEIGHT, 512) * factor


def solution(mesh):
    placed = (
        P("row", ("col", "layer")),
        P("col", "layer"),
        P("col", "layer"),
        P(("row", "col"), "layer"),
    )
    return jax.shard_map(
        shards, mesh=mesh, in_specs=placed, out_specs=P(("row", "col"), "layer"), check_vma=False
    )
```

```python
import jax
import jax.numpy as jnp
from jax import lax
from jax.experimental import pallas as pl
from jax.experimental.pallas import tpu as pltpu
from jax.sharding import PartitionSpec as P

BLOCK = 128
ROWS = 4096
SLABS = 16
HEIGHT = 1024 // SLABS
HALF = HEIGHT // 2
AHEAD = 3
LAG = 2
FORWARD_FROM = 5
PARTNER_FROM = 13
CODES = 65534.0
Z = 4
Y = 4
MESH = pl.DeviceIdType.MESH


def kernel(
    flow_ref,
    graph_ref,
    gp_ref,
    op_ref,
    out_ref,
    factor_ref,
    a,
    b_own,
    b_par,
    b_out,
    own,
    c1s,
    c1r,
    c2s,
    c2r,
    c3s,
    c3r,
    m1s,
    m1r,
    m2s,
    m2r,
    m3s,
    m3r,
    gp,
    op,
    sums,
    sums_in,
    g_send,
    g_recv,
    b_send,
    b_recv,
    f_send,
    f_recv,
    c_send,
    c_recv,
    m_send,
    m_recv,
    o_sem,
    t_send,
    t_recv,
    l_sem,
):
    core = lax.axis_index("row")
    xh = lax.axis_index("col")
    layer = lax.axis_index("layer")
    z = layer // 8
    y = lax.rem(layer // 2, 4)
    xl = lax.rem(layer, 2)
    yn = (lax.rem(y + 1, 4), lax.rem(y + 3, 4))
    zn = (lax.rem(z + 1, 4), lax.rem(z + 3, 4))

    def at(zz, yy, xxl):
        return zz * 8 + yy * 2 + xxl

    y_dev = tuple((core, xh, at(z, v, xl)) for v in yn)
    z_dev = tuple((core, xh, at(v, y, xl)) for v in zn)
    pair = (core, xh, at(z, y, 1 - xl))
    cross = (core, 1 - xh, at(z, y, 1 - xl))
    sibling = (1 - core, xh, layer)
    opposite = (core, 1 - xh, layer)
    diagonal = (1 - core, 1 - xh, layer)
    peers = (sibling, opposite, diagonal)

    barrier = pltpu.get_barrier_semaphore()
    for dev in (*y_dev, *z_dev, pair, cross, *peers):
        pl.semaphore_signal(barrier, inc=1, device_id=dev, device_id_type=MESH)

    load_a = pltpu.make_async_copy(flow_ref, a.at[:, :, z, y], l_sem.at[0])
    load_a.start()
    load_bo = pltpu.make_async_copy(graph_ref.at[pl.ds(core * 8, 8), 1 - xl], b_out, l_sem.at[1])
    load_bo.start()
    load_gp = pltpu.make_async_copy(gp_ref, gp, l_sem.at[3])
    load_gp.start()
    load_op = pltpu.make_async_copy(op_ref, op, l_sem.at[4])
    load_op.start()
    load_b = pltpu.make_async_copy(graph_ref.at[:, xl], b_own, l_sem.at[2])
    load_b.start()

    pl.semaphore_wait(barrier, 9)

    def gather_copy(stage, f, d, s):
        first = y_dev if f == 0 else z_dev
        second = z_dev if f == 0 else y_dev
        back = 1 - d
        rows = pl.ds(HALF * d, HALF)
        if stage == 0:
            ref, src, dev = a.at[f, s, z, y], flow_ref.at[f, s], first[d]
        elif stage == 1:
            ref = a.at[f, s, z, yn[back], rows] if f == 0 else a.at[f, s, zn[back], y, rows]
            dev = first[d]
        elif stage == 2:
            ref = a.at[f, s, z] if f == 0 else a.at[f, s, :, y]
            dev = second[d]
        else:
            ref = a.at[f, s, zn[back], :, rows] if f == 0 else a.at[f, s, :, yn[back], rows]
            dev = second[d]
        return pltpu.make_async_remote_copy(
            src_ref=src if stage == 0 else ref,
            dst_ref=ref,
            send_sem=g_send.at[stage, f, d, s],
            recv_sem=g_recv.at[stage, f, d, s],
            device_id=dev,
            device_id_type=MESH,
        )

    def remote(src, dst, send, recv, dev):
        return pltpu.make_async_remote_copy(
            src_ref=src, dst_ref=dst, send_sem=send, recv_sem=recv, device_id=dev, device_id_type=MESH
        )

    def issue(stage, s):
        for d in range(2):
            for f in range(2):
                if stage > 0:
                    if stage == 2 and d == 0:
                        gather_copy(1, f, 0, s).wait_recv()
                        gather_copy(1, f, 1, s).wait_recv()
                    elif stage != 2:
                        gather_copy(stage - 1, f, d, s).wait_recv()
                gather_copy(stage, f, d, s).start()

    def drain(s):
        for stage in range(4):
            for f in range(2):
                for d in range(2):
                    gather_copy(stage, f, d, s).wait_send()

    def b_copy(j):
        return remote(b_out.at[j], b_par.at[core * 8 + j], b_send.at[j], b_recv.at[j], pair)

    def f_copy(j):
        ref = b_par.at[core * 8 + j]
        return remote(ref, ref, f_send.at[j], f_recv.at[j], sibling)

    parts = ((c1s, c1r, m1s, m1r, cross), (c2s, c2r, m2s, m2r, pair), (c3s, c3r, m3s, m3r, cross))

    def c_copies(k, s, direct=False):
        src, dst, top, top_in, dev = parts[k]
        if direct:
            dev = opposite
        return (
            remote(src.at[s], dst.at[s], c_send.at[k, s], c_recv.at[k, s], dev),
            remote(top.at[s], top_in.at[s], m_send.at[k, s], m_recv.at[k, s], dev),
        )

    def encode(k, s, cols, v):
        top = jnp.maximum(v.max(axis=0, keepdims=True), 1e-30)
        code = (v * (CODES / top) + 0.5).astype(jnp.int32) - 32767
        parts[k][0][s, :, cols] = code.astype(jnp.int16)
        parts[k][2][s, :, cols] = top

    def decode(k, s, cols):
        code = parts[k][1][s, :, cols].astype(jnp.int32) + 32767
        return code.astype(jnp.float32) * (parts[k][3][s, :, cols] * (1.0 / CODES))

    def out_copy(s):
        return pltpu.make_async_copy(own.at[s], out_ref.at[s], o_sem.at[s])

    def mask(ref, j, chunk, x):
        for r in range(2):
            for c in range(4):
                keep = gp[c, (chunk * 2 + x) * 2 + r].astype(jnp.float32)
                keep = jnp.full((16, BLOCK), keep, jnp.float32).astype(jnp.bfloat16)
                rows, cols = pl.ds(r * BLOCK, BLOCK), pl.ds(c * BLOCK, BLOCK)
                block = ref[j, rows, cols].reshape(8, 16, BLOCK) * keep
                ref[j, rows, cols] = block.reshape(BLOCK, BLOCK)

    def rows_of(s):
        halves = []
        for h in (xh, 1 - xh):
            halves.append(jnp.concatenate([a[h, s, zz, yy] for zz in range(Z) for yy in range(Y)], axis=1))
        return jnp.concatenate(halves, axis=0)

    def product(s, b, n):
        cols = pl.ds(pl.multiple_of(n * 256, 256), 256)
        return jnp.dot(rows_of(s), b[:, :, cols].reshape(4096, 256), preferred_element_type=jnp.float32), cols

    def compute_own(s, direct=False):
        @pl.loop(0, 2)
        def _(n):
            r, cols = product(s, b_own, n)
            own[s, :, cols] = r[:HEIGHT]
            encode(0, s, cols, r[HEIGHT:])

        for copy in c_copies(0, s, direct):
            copy.start()

    def compute_par(s, direct=False):
        if not direct:
            for copy in c_copies(0, s):
                copy.wait_recv()

        @pl.loop(0, 2)
        def _(n):
            r, cols = product(s, b_par, n)
            encode(1, s, cols, r[:HEIGHT] if direct else r[:HEIGHT] + decode(0, s, cols))
            encode(2, s, cols, r[HEIGHT:])

        for k in (1, 2):
            for copy in c_copies(k, s):
                copy.start()

    def finish(s, direct=False):
        came = (1, 2, 0) if direct else (1, 2)
        for k in came:
            for copy in c_copies(k, s, direct and k == 0):
                copy.wait_recv()
        for c in range(4):
            cols = pl.ds(c * BLOCK, BLOCK)
            keep = op[c, s * HEIGHT // BLOCK].astype(jnp.float32)
            v = own[s, :, cols] + sum(decode(k, s, cols) for k in came)
            v = v * v * keep
            own[s, :, cols] = v
            sums[:, cols] += v.reshape(HEIGHT // 8, 8, BLOCK).sum(axis=0)
        out_copy(s).start()
        for k in range(3):
            for copy in c_copies(k, s, direct and k == 0):
                copy.wait_send()

    sums[...] = jnp.zeros_like(sums)

    issue(0, 0)
    load_bo.wait()
    load_gp.wait()
    load_op.wait()

    def send_b(j):
        mask(b_out, j, core * 8 + j, 1 - xl)
        b_copy(j).start()

    send_b(0)

    @pl.loop(1, AHEAD + 1)
    def _(s):
        issue(0, s)

    last = SLABS + 4 * LAG

    def par_end(t):
        return jnp.clip(jnp.minimum(t - 4 * LAG, 4 * (t - PARTNER_FROM + 1)), 0, SLABS)

    def fwd_end(t):
        return jnp.clip(t - FORWARD_FROM, 0, 8)

    @pl.loop(1, last)
    def _(t):
        for stage in (2, 3, 1, 0):
            s = t - LAG * stage + (AHEAD if stage == 0 else 0)

            @pl.when((s >= 0) & (s < SLABS))
            def _():
                issue(stage, s)

        @pl.when(t < 8)
        def _():
            send_b(t)

        @pl.when(t == 2)
        def _():
            load_a.wait()

        @pl.when(t == 4)
        def _():
            load_b.wait()

        @pl.when((t >= 4) & (t < 8))
        def _():
            @pl.loop(4 * (t - 4), 4 * (t - 3))
            def _(j):
                mask(b_own, j, j, xl)

        @pl.loop(fwd_end(t - 1), fwd_end(t))
        def _(j):
            b_copy(j).wait_recv()
            f_copy(j).start()

        @pl.when((t >= 4 * LAG) & (t < last - 1))
        def _():
            s = t - 4 * LAG
            for f in range(2):
                for d in range(2):
                    gather_copy(3, f, d, s).wait_recv()
            compute_own(s)

        @pl.when(t == PARTNER_FROM)
        def _():
            @pl.loop(0, 8)
            def _(j):
                f_copy(j).wait_recv()

        @pl.loop(par_end(t - 1), par_end(t))
        def _(s):
            compute_par(s)

        @pl.loop(par_end(t - 3), par_end(t - 2))
        def _(s):
            finish(s)

        @pl.when(t > 4 * LAG)
        def _():
            drain(t - 4 * LAG - 1)

        @pl.when(t == PARTNER_FROM + 1)
        def _():
            @pl.loop(0, 8)
            def _(j):
                b_copy(j).wait_send()
                f_copy(j).wait_send()

    for f in range(2):
        for d in range(2):
            gather_copy(3, f, d, SLABS - 1).wait_recv()
    compute_own(SLABS - 1, True)
    compute_par(SLABS - 1, True)

    @pl.loop(par_end(last - 3), SLABS - 1)
    def _(s):
        finish(s)

    finish(SLABS - 1, True)

    for k, dev in enumerate(peers):
        remote(sums, sums_in.at[k], t_send.at[k], t_recv.at[k], dev).start()

    drain(SLABS - 1)

    @pl.loop(0, SLABS)
    def _(s):
        out_copy(s).wait()

    for k, dev in enumerate(peers):
        remote(sums, sums_in.at[k], t_send.at[k], t_recv.at[k], dev).wait()
    total = sums[...] + sums_in[0] + sums_in[1] + sums_in[2]
    factor_ref[...] = jnp.float32(ROWS) / total.sum(axis=0, keepdims=True)


def shards(flow, graph, graph_pattern, out_pattern):
    f32, bf16 = jnp.float32, jnp.bfloat16
    dma = pltpu.SemaphoreType.DMA
    part = pltpu.VMEM((SLABS, HEIGHT, 512), jnp.int16)
    tops = pltpu.VMEM((SLABS, 1, 512), f32)
    inflated, factor = pl.pallas_call(
        kernel,
        out_shape=(
            jax.ShapeDtypeStruct((SLABS, HEIGHT, 512), f32),
            jax.ShapeDtypeStruct((1, 512), f32),
        ),
        in_specs=[
            pl.BlockSpec(memory_space=pl.ANY),
            pl.BlockSpec(memory_space=pl.ANY),
            pl.BlockSpec(memory_space=pl.ANY),
            pl.BlockSpec(memory_space=pl.ANY),
        ],
        out_specs=(pl.BlockSpec(memory_space=pl.ANY), pl.BlockSpec(memory_space=pltpu.VMEM)),
        scratch_shapes=[
            pltpu.VMEM((2, SLABS, Z, Y, HEIGHT, 256), bf16),
            pltpu.VMEM((16, 256, 512), bf16),
            pltpu.VMEM((16, 256, 512), bf16),
            pltpu.VMEM((8, 256, 512), bf16),
            pltpu.VMEM((SLABS, HEIGHT, 512), f32),
            part,
            part,
            part,
            part,
            part,
            part,
            tops,
            tops,
            tops,
            tops,
            tops,
            tops,
            pltpu.SMEM((4, 64), jnp.int32),
            pltpu.SMEM((4, 8), jnp.int32),
            pltpu.VMEM((8, 512), f32),
            pltpu.VMEM((3, 8, 512), f32),
            dma((4, 2, 2, SLABS)),
            dma((4, 2, 2, SLABS)),
            dma((8,)),
            dma((8,)),
            dma((8,)),
            dma((8,)),
            dma((3, SLABS)),
            dma((3, SLABS)),
            dma((3, SLABS)),
            dma((3, SLABS)),
            dma((SLABS,)),
            dma((3,)),
            dma((3,)),
            dma((5,)),
        ],
        compiler_params=pltpu.CompilerParams(
            collective_id=0, has_side_effects=True, vmem_limit_bytes=56 * 1024 * 1024
        ),
        cost_estimate=pl.CostEstimate(flops=2 * 2048 * 4096 * 1024, bytes_accessed=12 << 20, transcendentals=0),
    )(
        flow.reshape(2, SLABS, HEIGHT, 256),
        graph.reshape(16, 2, 256, 512),
        graph_pattern.T,
        out_pattern.T,
    )
    return inflated.reshape(SLABS * HEIGHT, 512) * factor


def solution(mesh):
    placed = (
        P("row", ("col", "layer")),
        P("col", "layer"),
        P("col", "layer"),
        P(("row", "col"), "layer"),
    )
    return jax.shard_map(
        shards, mesh=mesh, in_specs=placed, out_specs=P(("row", "col"), "layer"), check_vma=False
    )
```
